32 devices in a mesh: seq: 4 (over z), roll: 2 (over x), head: 4 (over y, core).
Axes of the slice: x: 2, y: 2, z: 4, core: 2. Of those that a mesh axis runs over, the one named last changes fastest.
Arguments:
- queries: bfloat16 [2, 768, 64, 128], P('roll', 'seq', 'head'), may hold values from -7 to 7
- rollout_keys: bfloat16 [2, 768, 8, 128], P('roll', 'seq', 'head'), may hold values from -6 to 6
- rollout_values: bfloat16 [2, 768, 8, 128], P('roll', 'seq', 'head'), may hold values from -24 to 24
- prompt_keys: bfloat16 [1024, 8, 128], P(('seq', 'roll'), 'head'), may hold values from -4.5 to 4.5
- prompt_values: bfloat16 [1024, 8, 128], P(('seq', 'roll'), 'head'), may hold values from -24 to 24
- grad_out: bfloat16 [2, 768, 64, 128], P('roll', 'seq', 'head'), may hold values from -24 to 24
- lengths: int32 [2], P('roll'), may hold values from 192 to 768, as said below
Outputs:
- attention_out: bfloat16 [2, 768, 64, 128], P('roll', 'seq', 'head')
- grad_queries: bfloat16 [2, 768, 64, 128], P('roll', 'seq', 'head')
- grad_rollout_keys: bfloat16 [2, 768, 8, 128], P('roll', 'seq', 'head')
- grad_rollout_values: bfloat16 [2, 768, 8, 128], P('roll', 'seq', 'head')
- grad_prompt_keys: bfloat16 [1024, 8, 128], P(('seq', 'roll'), 'head')
- grad_prompt_values: bfloat16 [1024, 8, 128], P(('seq', 'roll'), 'head')
The draws below stay inside these ranges and needn't reach their ends.
Inputs may be any that keep to these rules, and one draw needn't show every extreme that they name: `lengths`: every rollout's length is at least 192, and one rollout of each draw has all 768 positions live.
All inputs are finite; a program needn't handle non-finite values.
Results may differ from the reference program's by a relative error of at most 0.007.
Values may be sent and summed in bfloat16 or wider, within the bound.
No kernel may reach another device: no remote copies, remote signals or barrier semaphores. Data moves between devices by JAX's collectives and lax.ppermute only.
A program may use at most 128 MiB of HBM per device.

```python
import jax
import jax.numpy as jnp
from jax import lax

HD = 128
QH = 64
KVH = 8
R = 768
P_SIZE = 1024
ROLLS = 2


def draw_queries(key, part):
    key = jax.random.fold_in(key, 11)
    values = jnp.clip(1.5 * jax.random.normal(key, (ROLLS, R, QH, HD), jnp.float32), -7.0, 7.0)
    return values.astype(jnp.bfloat16)


def draw_prompt_keys(key, part):
    key = jax.random.fold_in(key, 23)
    values = jnp.clip(jax.random.normal(key, (P_SIZE, KVH, HD), jnp.float32), -4.5, 4.5)
    return values.astype(jnp.bfloat16)


def draw_lengths(key, part):
    key = jax.random.fold_in(key, 5)
    first_key, second_key = jax.random.split(key)
    full_member = jax.random.randint(first_key, (), 0, ROLLS)
    others = jax.random.randint(second_key, (ROLLS,), R // 4, R + 1)
    return jnp.where(jnp.arange(ROLLS) == full_member, R, others).astype(jnp.int32)


def level_of(key, dims, cuts, smallest, top_value):
    factor_of, own = 1.0, jax.random.fold_in(key, 6)
    for dim, parts in cuts:
        heights = jnp.exp(jax.random.uniform(jax.random.fold_in(own, dim), (parts,), jnp.float32, smallest / len(cuts), top_value / len(cuts)))
        factor_of = factor_of * jnp.repeat(heights, dims[dim] // parts).reshape([-1 if axis == dim else 1 for axis in range(len(dims))])
    return factor_of


def normal_values(rng, shape, spread, most, cuts=(), kind=jnp.bfloat16):
    values = jax.random.normal(rng, shape, jnp.float32) * spread
    if len(cuts) > 0:
        values = level_of(rng, shape, cuts, -0.22, 0.18) * values
    return jnp.clip(values, min=-most, max=most).astype(kind)


def setup_inputs(seed: int = 0) -> dict:
    keys = jax.random.split(jax.random.key(seed), 8)
    queries = draw_queries(jax.random.fold_in(keys[7], 71), 0)
    rollout_keys = normal_values(keys[1], (ROLLS, R, KVH, HD), 1.0, 6.0, ((0, 2), (1, 4), (2, 4)))
    rollout_values = normal_values(keys[2], (ROLLS, R, KVH, HD), 4.0, 24.0, ((0, 2), (1, 4), (2, 4)))
    prompt_keys = draw_prompt_keys(jax.random.fold_in(keys[7], 71), 0)
    prompt_values = normal_values(keys[4], (P_SIZE, KVH, HD), 4.0, 24.0, ((0, 8), (1, 4)))
    grad_out = normal_values(keys[5], (ROLLS, R, QH, HD), 4.0, 24.0, ((0, 2), (1, 4), (2, 4)))
    lengths = draw_lengths(jax.random.fold_in(keys[7], 71), 0)
    return {"queries": queries, "rollout_keys": rollout_keys, "rollout_values": rollout_values, "prompt_keys": prompt_keys, "prompt_values": prompt_values, "grad_out": grad_out, "lengths": lengths}


def rollout_pass(queries_one, keys_one, values_one, prompt_keys, prompt_values, cot_one, seq_length):
    total_rows = queries_one.shape[0]
    head_count = queries_one.shape[1]
    head_dim = queries_one.shape[2]
    group_count = keys_one.shape[1]
    per_group = head_count // group_count
    prompt_rows = prompt_keys.shape[0]
    all_keys = jnp.concatenate([prompt_keys, keys_one], axis=0).astype(jnp.float32)
    all_values = jnp.concatenate([prompt_values, values_one], axis=0).astype(jnp.float32)
    key_pos = jnp.concatenate([jnp.full((prompt_rows,), -1, jnp.int32), jnp.arange(total_rows, dtype=jnp.int32)])
    span_rows = min(256, total_rows)
    span_count = total_rows // span_rows
    score_scale = head_dim ** -0.5
    shaped_queries = queries_one.reshape(span_count, span_rows, group_count, per_group, head_dim)
    shaped_cot = cot_one.reshape(span_count, span_rows, group_count, per_group, head_dim)
    highest = lax.Precision.HIGHEST

    def one_span(carried, inputs):
        key_grads, value_grads = carried
        query_span, cot_span, span_index = inputs
        query_pos = span_index * span_rows + jnp.arange(span_rows, dtype=jnp.int32)
        query_float = query_span.astype(jnp.float32)
        scores = jnp.einsum('ngqd,kgd->gqnk', query_float, all_keys, precision=highest) * score_scale
        allowed = key_pos[None, :] <= query_pos[:, None]
        scores = jnp.where(allowed[None, None], scores, -jnp.inf)
        maxima = jnp.max(scores, -1)
        lifted = jnp.exp(scores - maxima[..., None])
        totals = jnp.sum(lifted, -1)
        lifted_low = lax.optimization_barrier(lifted.astype(jnp.bfloat16)).astype(jnp.float32)
        normalized = jnp.einsum('gqnk,kgd->gqnd', lifted_low, all_values, precision=highest) / totals[..., None]
        row_valid = query_pos < seq_length
        out_rows = jnp.where(row_valid[:, None, None, None], normalized.transpose(2, 0, 1, 3), 0.0)
        out_rows = out_rows.reshape(span_rows, head_count, head_dim).astype(jnp.bfloat16)
        log_total = maxima + jnp.log(totals)
        cot_live = jnp.where(row_valid[:, None, None, None], cot_span, jnp.zeros_like(cot_span)).astype(jnp.float32)
        offsets = jnp.sum(cot_live.transpose(1, 2, 0, 3) * normalized, -1)
        weights = jnp.exp(scores - log_total[..., None])
        grad_weights = jnp.einsum('ngqd,kgd->gqnk', cot_live, all_values, precision=highest)
        grad_scores = lax.optimization_barrier((weights * (grad_weights - offsets[..., None]) * score_scale).astype(jnp.bfloat16)).astype(jnp.float32)
        grad_query = jnp.einsum('gqnk,kgd->ngqd', grad_scores, all_keys, precision=highest)
        key_grads = key_grads + jnp.einsum('gqnk,ngqd->kgd', grad_scores, query_float, precision=highest)
        weights_low = lax.optimization_barrier(weights.astype(jnp.bfloat16)).astype(jnp.float32)
        value_grads = value_grads + jnp.einsum('gqnk,ngqd->kgd', weights_low, cot_live, precision=highest)
        grad_rows = grad_query.reshape(span_rows, head_count, head_dim).astype(jnp.bfloat16)
        return (key_grads, value_grads), (out_rows, grad_rows)

    zero_grads = jnp.zeros(all_keys.shape, jnp.float32)
    span_ids = jnp.arange(span_count, dtype=jnp.int32)
    (key_grads, value_grads), (out_spans, grad_spans) = lax.scan(one_span, (zero_grads, zero_grads), (shaped_queries, shaped_cot, span_ids))
    attention_one = out_spans.reshape(total_rows, head_count, head_dim)
    grad_one = grad_spans.reshape(total_rows, head_count, head_dim)
    return attention_one, grad_one, key_grads, value_grads


def reference(queries, rollout_keys, rollout_values, prompt_keys, prompt_values, grad_out, lengths):
    prompt_rows = prompt_keys.shape[0]
    results = [rollout_pass(queries[member], rollout_keys[member], rollout_values[member], prompt_keys, prompt_values, grad_out[member], lengths[member]) for member in range(ROLLS)]
    attention_out = jnp.stack([item[0] for item in results])
    grad_queries = jnp.stack([item[1] for item in results])
    grad_rollout_keys = jnp.stack([item[2][prompt_rows:] for item in results]).astype(jnp.bfloat16)
    grad_rollout_values = jnp.stack([item[3][prompt_rows:] for item in results]).astype(jnp.bfloat16)
    prompt_key_sum = results[0][2][:prompt_rows]
    prompt_value_sum = results[0][3][:prompt_rows]
    for item in results[1:]:
        prompt_key_sum = prompt_key_sum + item[2][:prompt_rows]
        prompt_value_sum = prompt_value_sum + item[3][:prompt_rows]
    return (attention_out, grad_queries, grad_rollout_keys, grad_rollout_values, prompt_key_sum.astype(jnp.bfloat16), prompt_value_sum.astype(jnp.bfloat16))
```

```python
import math

import jax
import jax.numpy as jnp
from jax import lax
from jax.experimental import pallas as pl
from jax.experimental.pallas import tpu as pltpu
from jax.sharding import PartitionSpec as P

BF16 = jnp.bfloat16
F32 = jnp.float32
LOG2E = math.log2(math.e)
VMEM = pl.BlockSpec(memory_space=pltpu.VMEM)
SMEM = pl.BlockSpec(memory_space=pltpu.SMEM)
HBM = pl.BlockSpec(memory_space=pltpu.HBM)


def dot_nn(a, b):
    return lax.dot_general(a, b, (((1,), (0,)), ((), ())), preferred_element_type=F32)


def dot_nt(a, b):
    return lax.dot_general(a, b, (((1,), (1,)), ((), ())), preferred_element_type=F32)


def params(mib=32):
    return pltpu.CompilerParams(vmem_limit_bytes=mib * 1024 * 1024)


def cost(flops, read_written, exps=0):
    return pl.CostEstimate(flops=flops, bytes_accessed=read_written, transcendentals=exps)


def load_all(refs, buffers, sems):
    copies = [pltpu.make_async_copy(ref, buffer, sems.at[i]) for i, (ref, buffer) in enumerate(zip(refs, buffers))]
    for copy in copies:
        copy.start()
    return copies


def split_heads(*arrays):
    groups, dim = arrays[0].shape[1:]
    starts = [0]
    for array in arrays:
        starts.append(starts[-1] + array.shape[0])

    def body(*refs):
        ins, outs = refs[: len(arrays)], refs[len(arrays) : len(arrays) + groups]
        buffers, sems = refs[len(arrays) + groups : -1], refs[-1]
        copies = load_all(ins, buffers, sems)
        for i, (copy, buffer) in enumerate(zip(copies, buffers)):
            copy.wait()
            wide = buffer[...].astype(F32)
            for g in range(groups):
                outs[g][starts[i] : starts[i + 1], :] = wide[:, g, :].astype(BF16)

    return pl.pallas_call(
        body,
        out_shape=[jax.ShapeDtypeStruct((starts[-1], dim), BF16)] * groups,
        in_specs=[HBM] * len(arrays),
        out_specs=[VMEM] * groups,
        scratch_shapes=[pltpu.VMEM(a.shape, BF16) for a in arrays] + [pltpu.SemaphoreType.DMA((len(arrays),))],
        compiler_params=params(63),
        cost_estimate=cost(0, 8 * starts[-1] * dim * groups),
    )(*arrays)


def split_queries(scalars, queries, grad_out, groups, own):
    rows, heads, dim = queries.shape
    per = heads // groups
    flat = rows * per

    def body(scalar_ref, q_ref, do_ref, *refs):
        own_refs, outs = refs[: len(own)], refs[len(own) :]
        wide = q_ref[...].astype(F32)
        for g in range(groups):
            outs[g][...] = wide[:, g * per : (g + 1) * per, :].reshape(flat, dim).astype(BF16)
        seen = lax.broadcasted_iota(jnp.int32, (rows, 1, 1), 0) < scalar_ref[0]
        wide = jnp.where(seen, do_ref[...].astype(F32), 0.0)
        for g in range(groups):
            outs[groups + g][...] = wide[:, g * per : (g + 1) * per, :].reshape(flat, dim).astype(BF16)
        for ref, out in zip(own_refs, outs[2 * groups :]):
            out[...] = ref[...]

    shapes = [jax.ShapeDtypeStruct((flat, dim), BF16)] * (2 * groups)
    shapes += [jax.ShapeDtypeStruct(item.shape, item.dtype) for item in own]
    outs = pl.pallas_call(
        body,
        out_shape=shapes,
        in_specs=[SMEM] + [VMEM] * (2 + len(own)),
        out_specs=[VMEM] * len(shapes),
        compiler_params=params(),
        cost_estimate=cost(0, 16 * rows * heads * dim),
    )(scalars, queries, grad_out, *own)
    return outs[:groups], outs[groups : 2 * groups], outs[2 * groups :]


def attend(scalars, queries, cotangent, prompts, rollouts, roll_size, block, first, end, carry):
    flat, dim = queries.shape
    seq_size = len(rollouts)
    prow, rrow = prompts[0][2] // 2, rollouts[0][2] // 2
    per = flat // rrow
    prompt_total = prow * seq_size * roll_size
    total = prompt_total + rrow * seq_size
    here = (end - first) * block
    opening, closing = first == 0, end * block == flat
    scale = dim ** (-0.5)
    exponent = scale * LOG2E
    sources, places = list(carry), []
    for array, at, rows in prompts + rollouts if opening else []:
        known = [i for i, seen in enumerate(sources) if seen is array]
        if not known:
            known = [len(sources)]
            sources.append(array)
        places.append((known[0], at, rows // 2))

    def body(*refs):
        scalar_ref, q_ref, do_ref = refs[:3]
        source_refs = refs[3 : 3 + len(sources)]
        out_ref, ds_ref = refs[3 + len(sources) : 5 + len(sources)]
        rest = list(refs[5 + len(sources) :])
        if opening:
            k_s, v_s = rest.pop(0), rest.pop(0)
        else:
            k_s, v_s = source_refs[:2]
        if closing:
            line_refs, grad_refs = rest[:roll_size], rest[roll_size : roll_size + seq_size]
        dk_s, dv_s = rest[-2:]
        live = scalar_ref[0]
        rank = scalar_ref[1]

        lower = 0
        for which, start, rows in places:
            k_s[lower : lower + rows, :] = source_refs[which][start : start + rows, :]
            v_s[lower : lower + rows, :] = source_refs[which][start + rows : start + 2 * rows, :]
            lower += rows
        if opening:
            dk_s[...] = jnp.zeros_like(dk_s)
            dv_s[...] = jnp.zeros_like(dv_s)
        else:
            dk_s[...] = source_refs[2][...]
            dv_s[...] = source_refs[3][...]

        column = lax.broadcasted_iota(jnp.int32, (1, rrow * seq_size), 1)
        key_at = column
        for slot in range(1, seq_size):
            key_at = jnp.where(column >= slot * rrow, column + (scalar_ref[1 + slot] - rank - slot) * rrow, key_at)

        def forward(step):
            span = slice(step * block, (step + 1) * block)
            row = (step * block + lax.broadcasted_iota(jnp.int32, (block, 1), 0)) // per
            q = q_ref[span, :]
            s_p = dot_nt(q, k_s[:prompt_total, :])
            s_r = dot_nt(q, k_s[prompt_total:, :])
            s_r = jnp.where(key_at <= row, s_r, -jnp.inf)
            top = jnp.maximum(jnp.max(s_p, axis=1, keepdims=True), jnp.max(s_r, axis=1, keepdims=True))
            e_p = jnp.exp2((s_p - top) * exponent)
            e_r = jnp.exp2((s_r - top) * exponent)
            sums = jnp.sum(e_p, axis=1, keepdims=True) + jnp.sum(e_r, axis=1, keepdims=True)
            p_p = e_p.astype(BF16)
            p_r = e_r.astype(BF16)
            o = (dot_nn(p_p, v_s[:prompt_total, :]) + dot_nn(p_r, v_s[prompt_total:, :])) / sums
            there = slice((step - first) * block, (step - first + 1) * block)
            out_ref[there, :] = jnp.where(row < live, o, 0.0).astype(BF16)
            cot = (do_ref[span, :].astype(F32) * (scale / sums)).astype(BF16)
            cot32 = cot.astype(F32)
            off = jnp.sum(cot32 * o, axis=1, keepdims=True)
            q_t = q.astype(F32).T.astype(BF16)
            cot_t = cot32.T.astype(BF16)
            return p_p, p_r, cot, off, q_t, cot_t

        def backward(step, state):
            there = slice((step - first) * block, (step - first + 1) * block)
            p_p, p_r, cot, off, q_t, cot_t = state
            dv_s[:, :prompt_total] += dot_nn(cot_t, p_p)
            dv_s[:, prompt_total:] += dot_nn(cot_t, p_r)
            ds_p = (p_p.astype(F32) * (dot_nt(cot, v_s[:prompt_total, :]) - off)).astype(BF16)
            ds_r = (p_r.astype(F32) * (dot_nt(cot, v_s[prompt_total:, :]) - off)).astype(BF16)
            ds_ref[there, :prompt_total] = ds_p
            ds_ref[there, prompt_total:] = ds_r
            dk_s[:, :prompt_total] += dot_nn(q_t, ds_p)
            dk_s[:, prompt_total:] += dot_nn(q_t, ds_r)

        state = forward(first)
        for step in range(first, end):
            ahead = forward(step + 1) if step + 1 < end else None
            backward(step, state)
            state = ahead
        if not closing:
            return

        dk = dk_s[...].T
        dv = dv_s[...].T * (1.0 / scale)
        for dx, ref in enumerate(line_refs):
            for slot in range(seq_size):
                lower = (dx * seq_size + slot) * prow
                at = 2 * slot * prow
                ref[at : at + prow, :] = dk[lower : lower + prow, :].astype(ref.dtype)
                ref[at + prow : at + 2 * prow, :] = dv[lower : lower + prow, :].astype(ref.dtype)
        for slot, ref in enumerate(grad_refs):
            lower = prompt_total + slot * rrow
            ref[:rrow, :] = dk[lower : lower + rrow, :].astype(ref.dtype)
            ref[rrow:, :] = dv[lower : lower + rrow, :].astype(ref.dtype)

    shapes = [((here, dim), BF16), ((here, total), BF16)]
    sums = [((dim, total), F32)] * 2
    if opening:
        shapes += [((total, dim), BF16)] * 2
    if closing:
        shapes += [((seq_size * 2 * prow, dim), BF16 if dx else F32) for dx in range(roll_size)]
        shapes += [((2 * rrow, dim), BF16 if slot else F32) for slot in range(seq_size)]
    else:
        shapes += sums
    outs = pl.pallas_call(
        body,
        out_shape=[jax.ShapeDtypeStruct(shape, kind) for shape, kind in shapes],
        in_specs=[SMEM] + [VMEM] * (2 + len(sources)),
        out_specs=[VMEM] * len(shapes),
        scratch_shapes=[pltpu.VMEM(shape, kind) for shape, kind in sums] if closing else [],
        compiler_params=params(),
        cost_estimate=cost(20 * here * total * dim, 16 * here * dim, here * total),
    )(scalars, queries, cotangent, *sources)
    part, rest = tuple(outs[:2]), list(outs[2:])
    if not closing:
        return part, rest
    keys, rest = (rest[0], rest[2:]) if opening else (carry[0], rest)
    return part, keys, rest[:roll_size], rest[roll_size:]


def row_outputs(heads, keys, rows, block):
    groups = len(heads)
    total, dim = keys[0].shape
    flat = sum(out.shape[0] for out, _ in heads[0])
    per = flat // rows
    arrays = [item for head in heads for part in head for item in part]
    where, at = [], 0
    for head in heads:
        where.append([])
        for out, _ in head:
            where[-1] += [(at, lower) for lower in range(0, out.shape[0], block)]
            at += 2

    def body(*refs):
        part_refs, k_refs = refs[: len(arrays)], refs[len(arrays) : len(arrays) + groups]
        attention_ref, dq_ref = refs[len(arrays) + groups :]
        for i in range(flat // block):
            there = slice(i * block // per, (i + 1) * block // per)
            outs, grads = [], []
            for places, k in zip(where, k_refs):
                at, lower = places[i]
                span = slice(lower, lower + block)
                outs.append(part_refs[at][span, :].astype(F32).reshape(block // per, per, dim))
                grads.append(dot_nn(part_refs[at + 1][span, :], k[...]).reshape(block // per, per, dim))
            attention_ref[there] = jnp.concatenate(outs, axis=1).astype(BF16)
            dq_ref[there] = jnp.concatenate(grads, axis=1).astype(BF16)

    return pl.pallas_call(
        body,
        out_shape=[jax.ShapeDtypeStruct((rows, per * groups, dim), BF16)] * 2,
        in_specs=[VMEM] * (len(arrays) + groups),
        out_specs=[VMEM] * 2,
        compiler_params=params(),
        cost_estimate=cost(4 * groups * flat * total * dim, 2 * groups * flat * total),
    )(*arrays, *keys)


def pair_sum(owns, received, seq_size):
    groups = len(owns)
    rows, dim = owns[0].shape
    part = rows // seq_size
    count = len(received[0])

    def body(*refs):
        own_refs, other_refs, outs = refs[:groups], refs[groups : groups * (1 + count)], refs[groups * (1 + count) :]
        for slot, out in enumerate(outs):
            span = slice(slot * part, (slot + 1) * part)
            for g, own_ref in enumerate(own_refs):
                value = own_ref[span, :]
                for other in other_refs[g * count : (g + 1) * count]:
                    value = value + other[span, :].astype(F32)
                out[g * part : (g + 1) * part, :] = value.astype(out.dtype)

    return pl.pallas_call(
        body,
        out_shape=[jax.ShapeDtypeStruct((groups * part, dim), BF16 if slot else F32) for slot in range(seq_size)],
        in_specs=[VMEM] * (groups * (1 + count)),
        out_specs=[VMEM] * seq_size,
        compiler_params=params(),
        cost_estimate=cost(groups * rows * dim, groups * rows * dim * 10),
    )(*owns, *[item for line in received for item in line])


def finish(owns, received, groups):
    each = groups // len(owns)
    dim = owns[0].shape[1]
    rows = owns[0].shape[0] // (2 * each)
    count = len(received[0])

    def body(*refs):
        own, rest = refs[: len(owns)], refs[len(owns) :]
        sums = []
        for g in range(groups):
            i, span = g // each, slice(g % each * 2 * rows, (g % each + 1) * 2 * rows)
            value = own[i][span, :]
            for other in rest[i * count : (i + 1) * count]:
                value = value + other[span, :].astype(F32)
            sums.append(value)
        for part, out in enumerate(refs[-2:]):
            pieces = [value[part * rows : (part + 1) * rows, None, :] for value in sums]
            out[...] = jnp.concatenate(pieces, axis=1).astype(BF16)

    flat = [item for line in received for item in line]
    return pl.pallas_call(
        body,
        out_shape=[jax.ShapeDtypeStruct((rows, groups, dim), BF16)] * 2,
        in_specs=[VMEM] * (len(owns) + len(flat)),
        out_specs=[VMEM] * 2,
        compiler_params=params(),
        cost_estimate=cost(2 * rows * groups * dim * count, 2 * rows * groups * dim * 10),
    )(*owns, *flat)


def after(value, *others):
    return lax.optimization_barrier((value, others))[0]


def local(queries, rollout_keys, rollout_values, prompt_keys, prompt_values, grad_out, lengths):
    seq_size, roll_size = lax.axis_size("seq"), lax.axis_size("roll")
    row_count, groups = queries.shape[1], prompt_keys.shape[1]
    flat = row_count * queries.shape[2] // groups
    rank = lax.axis_index("seq")
    paired = seq_size & (seq_size - 1) == 0
    slots = range(1, seq_size)
    origin = [(rank ^ slot) if paired else (rank - slot) % seq_size for slot in slots]
    scalars = jnp.stack([lengths[0] - rank * row_count, rank] + origin).astype(jnp.int32)

    def pairs(slot):
        return [(i, i ^ slot if paired else (i + slot) % seq_size) for i in range(seq_size)]

    def over_seq(value, which):
        return lax.ppermute(value, "seq", which)

    def give_back(value, slot):
        return over_seq(value, [(b, a) for a, b in pairs(slot)])

    def give_down(value, slot):
        return over_seq(value, [(b, a) for a, b in pairs(slot) if a < b])

    def over_roll(value, shift):
        return lax.ppermute(value, "roll", [(i, (i + shift) % roll_size) for i in range(roll_size)])

    own = split_heads(prompt_keys, prompt_values, rollout_keys[0], rollout_values[0])
    q_groups, cot_groups, kept = split_queries(scalars, queries[0], grad_out[0], groups, own)
    prows, rrows = 2 * prompt_keys.shape[0], 2 * row_count

    def send_over_seq(part, same):
        return [same] + [over_seq(part, pairs(slot)) for slot in slots]

    def send_over_roll(messages):
        line = jnp.concatenate([item[:prows] for item in messages], axis=0)
        return [line] + [over_roll(line, shift) for shift in range(1, roll_size)]

    messages = send_over_seq(own[0], kept[0])
    lines = send_over_roll(messages)
    block = math.gcd(flat, 256)
    steps = flat // block
    heads, all_keys, line_own, line_got, roll_own, roll_got = [], [], [], [], [], []
    for g in range(groups):
        prompts = [(item, slot * prows, prows) for item in lines for slot in range(seq_size)]
        rollouts = [(item, prows, rrows) for item in messages]
        if g + 1 < groups:
            messages = send_over_seq(after(own[g + 1], lines[0]), kept[g + 1])
        cuts = [0, steps // 2, steps] if g else [0, steps]
        parts, carry = [], []
        for start, stop in zip(cuts, cuts[1:]):
            if start:
                carry = [after(item, roll_got[g - 1]) for item in carry]
            part, *rest = attend(
                scalars, q_groups[g], cot_groups[g], prompts, rollouts, roll_size, block, start, stop, carry
            )
            parts.append(part)
            carry = rest[0]
        keys, line_grads, roll_grads = rest
        heads.append(parts)
        all_keys.append(keys)
        line_own.append(line_grads[0])
        line_got.append([over_roll(line_grads[shift], -shift) for shift in range(1, roll_size)])
        if g + 1 < groups:
            messages = [after(item, parts) for item in messages]
            lines = send_over_roll(messages)
            roll_grads = [after(item, lines[0]) for item in roll_grads]
        roll_own.append(roll_grads[0])
        roll_got.append([give_down(roll_grads[slot], slot) for slot in slots])

    sums = pair_sum(line_own, line_got, seq_size)
    attention_rows, grad_rows = row_outputs(heads, all_keys, row_count, block)
    grad_rk, grad_rv = finish(roll_own, roll_got, groups)
    grad_pk, grad_pv = finish([sums[0]], [[give_back(sums[slot], slot) for slot in slots]], groups)
    return attention_rows[None], grad_rows[None], grad_rk[None], grad_rv[None], grad_pk, grad_pv


def solution(mesh):
    rows = P("roll", "seq", "head", None)
    shared = P(("seq", "roll"), "head", None)
    return jax.shard_map(
        local,
        mesh=mesh,
        in_specs=(rows, rows, rows, shared, shared, rows, P("roll")),
        out_specs=(rows, rows, rows, rows, shared, shared),
        check_vma=False,
    )
```

```python
import math

import jax
import jax.numpy as jnp
from jax import lax
from jax.experimental import pallas as pl
from jax.experimental.pallas import tpu as pltpu
from jax.sharding import PartitionSpec as P

BF16 = jnp.bfloat16
F32 = jnp.float32
LOG2E = math.log2(math.e)
VMEM = pl.BlockSpec(memory_space=pltpu.VMEM)
SMEM = pl.BlockSpec(memory_space=pltpu.SMEM)
HBM = pl.BlockSpec(memory_space=pltpu.HBM)


def dot_nn(a, b):
    return lax.dot_general(a, b, (((1,), (0,)), ((), ())), preferred_element_type=F32)


def dot_nt(a, b):
    return lax.dot_general(a, b, (((1,), (1,)), ((), ())), preferred_element_type=F32)


def params(mib=32):
    return pltpu.CompilerParams(vmem_limit_bytes=mib * 1024 * 1024)


def cost(flops, read_written, exps=0):
    return pl.CostEstimate(flops=flops, bytes_accessed=read_written, transcendentals=exps)


def load_all(refs, buffers, sems):
    copies = [pltpu.make_async_copy(ref, buffer, sems.at[i]) for i, (ref, buffer) in enumerate(zip(refs, buffers))]
    for copy in copies:
        copy.start()
    return copies


def split_heads(*arrays):
    groups, dim = arrays[0].shape[1:]
    starts = [0]
    for array in arrays:
        starts.append(starts[-1] + array.shape[0])

    def body(*refs):
        ins, outs = refs[: len(arrays)], refs[len(arrays) : len(arrays) + groups]
        buffers, sems = refs[len(arrays) + groups : -1], refs[-1]
        copies = load_all(ins, buffers, sems)
        for i, (copy, buffer) in enumerate(zip(copies, buffers)):
            copy.wait()
            wide = buffer[...].astype(F32)
            for g in range(groups):
                outs[g][starts[i] : starts[i + 1], :] = wide[:, g, :].astype(BF16)

    return pl.pallas_call(
        body,
        out_shape=[jax.ShapeDtypeStruct((starts[-1], dim), BF16)] * groups,
        in_specs=[HBM] * len(arrays),
        out_specs=[VMEM] * groups,
        scratch_shapes=[pltpu.VMEM(a.shape, BF16) for a in arrays] + [pltpu.SemaphoreType.DMA((len(arrays),))],
        compiler_params=params(63),
        cost_estimate=cost(0, 8 * starts[-1] * dim * groups),
    )(*arrays)


def split_queries(scalars, queries, grad_out, groups, own):
    rows, heads, dim = queries.shape
    per = heads // groups
    flat = rows * per

    def body(scalar_ref, q_ref, do_ref, *refs):
        own_refs, outs = refs[: len(own)], refs[len(own) :]
        wide = q_ref[...].astype(F32)
        for g in range(groups):
            outs[g][...] = wide[:, g * per : (g + 1) * per, :].reshape(flat, dim).astype(BF16)
        seen = lax.broadcasted_iota(jnp.int32, (rows, 1, 1), 0) < scalar_ref[0]
        wide = jnp.where(seen, do_ref[...].astype(F32), 0.0)
        for g in range(groups):
            outs[groups + g][...] = wide[:, g * per : (g + 1) * per, :].reshape(flat, dim).astype(BF16)
        for ref, out in zip(own_refs, outs[2 * groups :]):
            out[...] = ref[...]

    shapes = [jax.ShapeDtypeStruct((flat, dim), BF16)] * (2 * groups)
    shapes += [jax.ShapeDtypeStruct(item.shape, item.dtype) for item in own]
    outs = pl.pallas_call(
        body,
        out_shape=shapes,
        in_specs=[SMEM] + [VMEM] * (2 + len(own)),
        out_specs=[VMEM] * len(shapes),
        compiler_params=params(),
        cost_estimate=cost(0, 16 * rows * heads * dim),
    )(scalars, queries, grad_out, *own)
    return outs[:groups], outs[groups : 2 * groups], outs[2 * groups :]


def attend(scalars, queries, cotangent, prompts, rollouts, roll_size, bundles, block, first, end, carry):
    flat, dim = queries.shape
    seq_size = len(rollouts)
    prow, rrow = prompts[0][2] // 2, rollouts[0][2] // 2
    per = flat // rrow
    prompt_total = prow * seq_size * roll_size
    total = prompt_total + rrow * seq_size
    here = (end - first) * block
    opening, closing = first == 0, end * block == flat
    scale = dim ** (-0.5)
    exponent = scale * LOG2E
    sources, places = list(carry), []
    for array, at, rows in prompts + rollouts if opening else []:
        known = [i for i, seen in enumerate(sources) if seen is array]
        if not known:
            known = [len(sources)]
            sources.append(array)
        places.append((known[0], at, rows // 2))

    def body(*refs):
        scalar_ref, q_ref, do_ref = refs[:3]
        source_refs = refs[3 : 3 + len(sources)]
        out_ref, ds_ref = refs[3 + len(sources) : 5 + len(sources)]
        rest = list(refs[5 + len(sources) :])
        if opening:
            k_s, v_s = rest.pop(0), rest.pop(0)
        else:
            k_s, v_s = source_refs[:2]
        if closing:
            line_refs, grad_refs = rest[:roll_size], rest[roll_size : roll_size + len(bundles)]
        dk_s, dv_s = rest[-2:]
        live = scalar_ref[0]
        rank = scalar_ref[1]

        lower = 0
        for which, start, rows in places:
            k_s[lower : lower + rows, :] = source_refs[which][start : start + rows, :]
            v_s[lower : lower + rows, :] = source_refs[which][start + rows : start + 2 * rows, :]
            lower += rows
        if opening:
            dk_s[...] = jnp.zeros_like(dk_s)
            dv_s[...] = jnp.zeros_like(dv_s)
        else:
            dk_s[...] = source_refs[2][...]
            dv_s[...] = source_refs[3][...]

        column = lax.broadcasted_iota(jnp.int32, (1, rrow * seq_size), 1)
        key_at = column
        for slot in range(1, seq_size):
            key_at = jnp.where(column >= slot * rrow, column + (scalar_ref[1 + slot] - rank - slot) * rrow, key_at)

        def forward(step):
            span = slice(step * block, (step + 1) * block)
            row = (step * block + lax.broadcasted_iota(jnp.int32, (block, 1), 0)) // per
            q = q_ref[span, :]
            s_p = dot_nt(q, k_s[:prompt_total, :])
            s_r = dot_nt(q, k_s[prompt_total:, :])
            s_r = jnp.where(key_at <= row, s_r, -jnp.inf)
            top = jnp.maximum(jnp.max(s_p, axis=1, keepdims=True), jnp.max(s_r, axis=1, keepdims=True))
            e_p = jnp.exp2((s_p - top) * exponent)
            e_r = jnp.exp2((s_r - top) * exponent)
            sums = jnp.sum(e_p, axis=1, keepdims=True) + jnp.sum(e_r, axis=1, keepdims=True)
            p_p = e_p.astype(BF16)
            p_r = e_r.astype(BF16)
            o = (dot_nn(p_p, v_s[:prompt_total, :]) + dot_nn(p_r, v_s[prompt_total:, :])) / sums
            there = slice((step - first) * block, (step - first + 1) * block)
            out_ref[there, :] = jnp.where(row < live, o, 0.0).astype(BF16)
            cot = (do_ref[span, :].astype(F32) * (scale / sums)).astype(BF16)
            cot32 = cot.astype(F32)
            off = jnp.sum(cot32 * o, axis=1, keepdims=True)
            q_t = q.astype(F32).T.astype(BF16)
            cot_t = cot32.T.astype(BF16)
            return p_p, p_r, cot, off, q_t, cot_t

        def backward(step, state):
            there = slice((step - first) * block, (step - first + 1) * block)
            p_p, p_r, cot, off, q_t, cot_t = state
            dv_s[:, :prompt_total] += dot_nn(cot_t, p_p)
            dv_s[:, prompt_total:] += dot_nn(cot_t, p_r)
            ds_p = (p_p.astype(F32) * (dot_nt(cot, v_s[:prompt_total, :]) - off)).astype(BF16)
            ds_r = (p_r.astype(F32) * (dot_nt(cot, v_s[prompt_total:, :]) - off)).astype(BF16)
            ds_ref[there, :prompt_total] = ds_p
            ds_ref[there, prompt_total:] = ds_r
            dk_s[:, :prompt_total] += dot_nn(q_t, ds_p)
            dk_s[:, prompt_total:] += dot_nn(q_t, ds_r)

        state = forward(first)
        for step in range(first, end):
            ahead = forward(step + 1) if step + 1 < end else None
            backward(step, state)
            state = ahead
        if not closing:
            return

        dk = dk_s[...].T
        dv = dv_s[...].T * (1.0 / scale)
        for dx, ref in enumerate(line_refs):
            for slot in range(seq_size):
                lower = (dx * seq_size + slot) * prow
                at = 2 * slot * prow
                ref[at : at + prow, :] = dk[lower : lower + prow, :].astype(ref.dtype)
                ref[at + prow : at + 2 * prow, :] = dv[lower : lower + prow, :].astype(ref.dtype)
        for (members, _), ref in zip(bundles, grad_refs):
            for i, slot in enumerate(members):
                lower, at = prompt_total + slot * rrow, 2 * i * rrow
                ref[at : at + rrow, :] = dk[lower : lower + rrow, :].astype(ref.dtype)
                ref[at + rrow : at + 2 * rrow, :] = dv[lower : lower + rrow, :].astype(ref.dtype)

    shapes = [((here, dim), BF16), ((here, total), BF16)]
    sums = [((dim, total), F32)] * 2
    if opening:
        shapes += [((total, dim), BF16)] * 2
    if closing:
        shapes += [((seq_size * 2 * prow, dim), BF16 if dx else F32) for dx in range(roll_size)]
        shapes += [((2 * rrow * len(members), dim), kind) for members, kind in bundles]
    else:
        shapes += sums
    outs = pl.pallas_call(
        body,
        out_shape=[jax.ShapeDtypeStruct(shape, kind) for shape, kind in shapes],
        in_specs=[SMEM] + [VMEM] * (2 + len(sources)),
        out_specs=[VMEM] * len(shapes),
        scratch_shapes=[pltpu.VMEM(shape, kind) for shape, kind in sums] if closing else [],
        compiler_params=params(),
        cost_estimate=cost(20 * here * total * dim, 16 * here * dim, here * total),
    )(scalars, queries, cotangent, *sources)
    part, rest = tuple(outs[:2]), list(outs[2:])
    if not closing:
        return part, rest if opening else list(carry[:2]) + rest
    keys, rest = (rest[0], rest[2:]) if opening else (carry[0], rest)
    return part, keys, rest[:roll_size], rest[roll_size:]


def row_outputs(heads, keys, rows, block):
    groups = len(heads)
    total, dim = keys[0].shape
    flat = sum(out.shape[0] for out, _ in heads[0])
    per = flat // rows
    arrays = [item for head in heads for part in head for item in part]
    where, at = [], 0
    for head in heads:
        where.append([])
        for out, _ in head:
            where[-1] += [(at, lower) for lower in range(0, out.shape[0], block)]
            at += 2

    def body(*refs):
        part_refs, k_refs = refs[: len(arrays)], refs[len(arrays) : len(arrays) + groups]
        attention_ref, dq_ref = refs[len(arrays) + groups :]
        for i in range(flat // block):
            there = slice(i * block // per, (i + 1) * block // per)
            outs, grads = [], []
            for places, k in zip(where, k_refs):
                at, lower = places[i]
                span = slice(lower, lower + block)
                outs.append(part_refs[at][span, :].astype(F32).reshape(block // per, per, dim))
                grads.append(dot_nn(part_refs[at + 1][span, :], k[...]).reshape(block // per, per, dim))
            attention_ref[there] = jnp.concatenate(outs, axis=1).astype(BF16)
            dq_ref[there] = jnp.concatenate(grads, axis=1).astype(BF16)

    return pl.pallas_call(
        body,
        out_shape=[jax.ShapeDtypeStruct((rows, per * groups, dim), BF16)] * 2,
        in_specs=[VMEM] * (len(arrays) + groups),
        out_specs=[VMEM] * 2,
        compiler_params=params(),
        cost_estimate=cost(4 * groups * flat * total * dim, 2 * groups * flat * total),
    )(*arrays, *keys)


def pair_sum(own, received, bundles, seq_size):
    rows, dim = own.shape
    part = rows // seq_size
    count = len(received)

    def body(own_ref, *refs):
        others, outs = refs[:count], refs[count:]
        for (members, _), out in zip(bundles, outs):
            for i, slot in enumerate(members):
                span = slice(slot * part, (slot + 1) * part)
                value = own_ref[span, :]
                for other in others:
                    value = value + other[span, :].astype(F32)
                out[i * part : (i + 1) * part, :] = value.astype(out.dtype)

    return pl.pallas_call(
        body,
        out_shape=[jax.ShapeDtypeStruct((part * len(members), dim), kind) for members, kind in bundles],
        in_specs=[VMEM] * (1 + count),
        out_specs=[VMEM] * len(bundles),
        compiler_params=params(),
        cost_estimate=cost(rows * dim, rows * dim * 10),
    )(own, *received)


def fold(bundled, received):
    count = len(bundled)
    rows, dim = bundled[0][0].shape

    def body(*refs):
        owns, theirs, came = refs[:count], refs[count : 2 * count], refs[2 * count : 3 * count]
        kept_ref, sent_ref = refs[3 * count :]
        for i in range(count):
            span = slice(i * rows, (i + 1) * rows)
            kept_ref[span, :] = owns[i][...] + came[i][:rows, :].astype(F32)
            sent_ref[span, :] = (theirs[i][...] + came[i][rows:, :].astype(F32)).astype(BF16)

    return pl.pallas_call(
        body,
        out_shape=[jax.ShapeDtypeStruct((count * rows, dim), kind) for kind in (F32, BF16)],
        in_specs=[VMEM] * (3 * count),
        out_specs=[VMEM] * 2,
        compiler_params=params(),
        cost_estimate=cost(2 * count * rows * dim, count * rows * dim * 18),
    )(*[item[0] for item in bundled], *[item[2] for item in bundled], *received)


def finish(owns, received, groups):
    each = groups // len(owns)
    dim = owns[0].shape[1]
    rows = owns[0].shape[0] // (2 * each)
    count = len(received[0])

    def body(*refs):
        own, rest = refs[: len(owns)], refs[len(owns) :]
        sums = []
        for g in range(groups):
            i, span = g // each, slice(g % each * 2 * rows, (g % each + 1) * 2 * rows)
            value = own[i][span, :]
            for other in rest[i * count : (i + 1) * count]:
                value = value + other[span, :].astype(F32)
            sums.append(value)
        for part, out in enumerate(refs[-2:]):
            pieces = [value[part * rows : (part + 1) * rows, None, :] for value in sums]
            out[...] = jnp.concatenate(pieces, axis=1).astype(BF16)

    flat = [item for line in received for item in line]
    return pl.pallas_call(
        body,
        out_shape=[jax.ShapeDtypeStruct((rows, groups, dim), BF16)] * 2,
        in_specs=[VMEM] * (len(owns) + len(flat)),
        out_specs=[VMEM] * 2,
        compiler_params=params(),
        cost_estimate=cost(2 * rows * groups * dim * count, 2 * rows * groups * dim * 10),
    )(*owns, *flat)


def after(value, *others):
    return lax.optimization_barrier((value, others))[0]


def local(queries, rollout_keys, rollout_values, prompt_keys, prompt_values, grad_out, lengths):
    seq_size, roll_size = lax.axis_size("seq"), lax.axis_size("roll")
    row_count, groups = queries.shape[1], prompt_keys.shape[1]
    flat = row_count * queries.shape[2] // groups
    rank = lax.axis_index("seq")
    paired = seq_size & (seq_size - 1) == 0
    slots = range(1, seq_size)
    origin = [(rank ^ slot) if paired else (rank - slot) % seq_size for slot in slots]
    scalars = jnp.stack([lengths[0] - rank * row_count, rank] + origin).astype(jnp.int32)

    def pairs(slot):
        return [(i, i ^ slot if paired else (i + slot) % seq_size) for i in range(seq_size)]

    def over_seq(value, which):
        return lax.ppermute(value, "seq", which)

    halving = seq_size == 4
    if halving:
        bundles = [((0,), F32), ((1, 3), BF16), ((2,), F32)]
    else:
        bundles = [((0,), F32)] + [((slot,), BF16) for slot in slots]

    def give(bundled, down):
        came = []
        for (members, kind), value in zip(bundles, bundled):
            if kind == BF16:
                back = [(b, a) for a, b in pairs(members[0])]
                if down:
                    back = [(a, b) for a, b in back if b < a or (len(members) > 1 and a ^ members[1] < a)]
                came.append(over_seq(value, back))
        return came

    def give_far(value, down):
        return over_seq(value, [(a, b) for a, b in pairs(2) if b < a or not down])

    def over_roll(value, shift):
        return lax.ppermute(value, "roll", [(i, (i + shift) % roll_size) for i in range(roll_size)])

    own = split_heads(prompt_keys, prompt_values, rollout_keys[0], rollout_values[0])
    q_groups, cot_groups, kept = split_queries(scalars, queries[0], grad_out[0], groups, own)
    prows, rrows = 2 * prompt_keys.shape[0], 2 * row_count

    def send_over_seq(part, same):
        return [same] + [over_seq(part, pairs(slot)) for slot in slots]

    def send_over_roll(messages):
        line = jnp.concatenate([item[:prows] for item in messages], axis=0)
        return [line] + [over_roll(line, shift) for shift in range(1, roll_size)]

    messages = send_over_seq(own[0], kept[0])
    lines = send_over_roll(messages)
    block = math.gcd(flat, 256)
    steps = flat // block
    heads, all_keys, prompt_sums, prompt_came, row_sums, row_came = [], [], [], [], [], []

    def settle_rows(sums, came):
        if halving:
            mine, sent = fold([sums], came)
            row_sums.append(mine)
            row_came.append([give_far(sent, True)])
        else:
            row_sums.append(sums[0])
            row_came.append(came)

    def settle_prompt(line_grads, came):
        prompt_sums.append(pair_sum(line_grads[0], came, bundles, seq_size))
        prompt_came.append(give(prompt_sums[-1], False))

    def back_over_roll(line_grads):
        return [over_roll(line_grads[shift], -shift) for shift in range(1, roll_size)]

    waiting = None
    for g in range(groups):
        prompts = [(item, slot * prows, prows) for item in lines for slot in range(seq_size)]
        rollouts = [(item, prows, rrows) for item in messages]
        if g + 1 < groups:
            messages = send_over_seq(after(own[g + 1], lines[0]), kept[g + 1])
        cuts = sorted({0, 1, steps - 1, steps}) if g else [0, steps]
        parts, carry = [], []
        for start, stop in zip(cuts, cuts[1:]):
            if waiting and start:
                sums, came, line_grads = waiting
                settle_rows(sums, [after(item, parts) for item in came])
                line_grads = [after(item, parts) for item in line_grads]
                line_came = back_over_roll(line_grads)
                waiting = None
            elif start:
                carry = [after(item, row_came[-1], line_came) for item in carry]
            part, *rest = attend(
                scalars, q_groups[g], cot_groups[g], prompts, rollouts, roll_size, bundles, block, start, stop, carry
            )
            parts.append(part)
            carry = rest[0]
        if g:
            settle_prompt(line_grads, line_came)
        keys, line_grads, roll_grads = rest
        heads.append(parts)
        all_keys.append(keys)
        if g + 1 < groups:
            messages = [after(item, parts) for item in messages]
            lines = send_over_roll(messages)
            roll_grads = [after(item, lines[0]) for item in roll_grads]
        waiting = (roll_grads, give(roll_grads, True), line_grads)
    settle_rows(*waiting[:2])
    settle_prompt(line_grads, back_over_roll(line_grads))

    attention_rows, grad_rows = row_outputs(heads, all_keys, row_count, block)
    grad_rk, grad_rv = finish(row_sums, row_came, groups)
    if halving:
        summed, sent = fold(prompt_sums, [came[0] for came in prompt_came])
        grad_pk, grad_pv = finish([summed], [[give_far(sent, False)]], groups)
    else:
        grad_pk, grad_pv = finish([sums[0] for sums in prompt_sums], prompt_came, groups)
    return attention_rows[None], grad_rows[None], grad_rk[None], grad_rv[None], grad_pk, grad_pv


def solution(mesh):
    rows = P("roll", "seq", "head", None)
    shared = P(("seq", "roll"), "head", None)
    return jax.shard_map(
        local,
        mesh=mesh,
        in_specs=(rows, rows, rows, shared, shared, rows, P("roll")),
        out_specs=(rows, rows, rows, rows, shared, shared),
        check_vma=False,
    )
```

```python
import math

import jax
import jax.numpy as jnp
from jax import lax
from jax.experimental import pallas as pl
from jax.experimental.pallas import tpu as pltpu
from jax.sharding import PartitionSpec as P

BF16 = jnp.bfloat16
F32 = jnp.float32
LOG2E = math.log2(math.e)
VMEM = pl.BlockSpec(memory_space=pltpu.VMEM)
SMEM = pl.BlockSpec(memory_space=pltpu.SMEM)
HBM = pl.BlockSpec(memory_space=pltpu.HBM)


def dot_nn(a, b):
    return lax.dot_general(a, b, (((1,), (0,)), ((), ())), preferred_element_type=F32)


def dot_nt(a, b):
    return lax.dot_general(a, b, (((1,), (1,)), ((), ())), preferred_element_type=F32)


def params(mib=32):
    return pltpu.CompilerParams(vmem_limit_bytes=mib * 1024 * 1024)


def cost(flops, read_written, exps=0):
    return pl.CostEstimate(flops=flops, bytes_accessed=read_written, transcendentals=exps)


def load_all(refs, buffers, sems):
    copies = [pltpu.make_async_copy(ref, buffer, sems.at[i]) for i, (ref, buffer) in enumerate(zip(refs, buffers))]
    for copy in copies:
        copy.start()
    return copies


def split_heads(*arrays):
    groups, dim = arrays[0].shape[1:]
    starts = [0]
    for array in arrays:
        starts.append(starts[-1] + array.shape[0])

    def body(*refs):
        ins, outs = refs[: len(arrays)], refs[len(arrays) : len(arrays) + groups]
        buffers, sems = refs[len(arrays) + groups : -1], refs[-1]
        copies = load_all(ins, buffers, sems)
        for i, (copy, buffer) in enumerate(zip(copies, buffers)):
            copy.wait()
            wide = buffer[...].astype(F32)
            for g in range(groups):
                outs[g][starts[i] : starts[i + 1], :] = wide[:, g, :].astype(BF16)

    return pl.pallas_call(
        body,
        out_shape=[jax.ShapeDtypeStruct((starts[-1], dim), BF16)] * groups,
        in_specs=[HBM] * len(arrays),
        out_specs=[VMEM] * groups,
        scratch_shapes=[pltpu.VMEM(a.shape, BF16) for a in arrays] + [pltpu.SemaphoreType.DMA((len(arrays),))],
        compiler_params=params(63),
        cost_estimate=cost(0, 8 * starts[-1] * dim * groups),
    )(*arrays)


def split_queries(scalars, queries, grad_out, groups, own):
    rows, heads, dim = queries.shape
    per = heads // groups
    flat = rows * per

    def body(scalar_ref, q_ref, do_ref, *refs):
        own_refs, outs = refs[: len(own)], refs[len(own) :]
        wide = q_ref[...].astype(F32)
        for g in range(groups):
            outs[g][...] = wide[:, g * per : (g + 1) * per, :].reshape(flat, dim).astype(BF16)
        seen = lax.broadcasted_iota(jnp.int32, (rows, 1, 1), 0) < scalar_ref[0]
        wide = jnp.where(seen, do_ref[...].astype(F32), 0.0)
        for g in range(groups):
            outs[groups + g][...] = wide[:, g * per : (g + 1) * per, :].reshape(flat, dim).astype(BF16)
        for ref, out in zip(own_refs, outs[2 * groups :]):
            out[...] = ref[...]

    shapes = [jax.ShapeDtypeStruct((flat, dim), BF16)] * (2 * groups)
    shapes += [jax.ShapeDtypeStruct(item.shape, item.dtype) for item in own]
    outs = pl.pallas_call(
        body,
        out_shape=shapes,
        in_specs=[SMEM] + [VMEM] * (2 + len(own)),
        out_specs=[VMEM] * len(shapes),
        compiler_params=params(),
        cost_estimate=cost(0, 16 * rows * heads * dim),
    )(scalars, queries, grad_out, *own)
    return outs[:groups], outs[groups : 2 * groups], outs[2 * groups :]


def attend(scalars, queries, cotangent, prompts, rollouts, roll_size, block, first, end, carry):
    flat, dim = queries.shape
    seq_size = len(rollouts)
    prow, rrow = prompts[0][2] // 2, rollouts[0][2] // 2
    per = flat // rrow
    prompt_total = prow * seq_size * roll_size
    total = prompt_total + rrow * seq_size
    here = (end - first) * block
    opening, closing = first == 0, end * block == flat
    scale = dim ** (-0.5)
    exponent = scale * LOG2E
    sources, places = list(carry), []
    for array, at, rows in prompts + rollouts if opening else []:
        known = [i for i, seen in enumerate(sources) if seen is array]
        if not known:
            known = [len(sources)]
            sources.append(array)
        places.append((known[0], at, rows // 2))

    def body(*refs):
        scalar_ref, q_ref, do_ref = refs[:3]
        source_refs = refs[3 : 3 + len(sources)]
        out_ref, ds_ref = refs[3 + len(sources) : 5 + len(sources)]
        rest = list(refs[5 + len(sources) :])
        if opening:
            k_s, v_s = rest.pop(0), rest.pop(0)
        else:
            k_s, v_s = source_refs[:2]
        if closing:
            line_refs, grad_refs = rest[:roll_size], rest[roll_size : roll_size + seq_size]
        dk_s, dv_s = rest[-2:]
        live = scalar_ref[0]
        rank = scalar_ref[1]

        lower = 0
        for which, start, rows in places:
            k_s[lower : lower + rows, :] = source_refs[which][start : start + rows, :]
            v_s[lower : lower + rows, :] = source_refs[which][start + rows : start + 2 * rows, :]
            lower += rows
        if opening:
            dk_s[...] = jnp.zeros_like(dk_s)
            dv_s[...] = jnp.zeros_like(dv_s)
        else:
            dk_s[...] = source_refs[2][...]
            dv_s[...] = source_refs[3][...]

        column = lax.broadcasted_iota(jnp.int32, (1, rrow * seq_size), 1)
        key_at = column
        for slot in range(1, seq_size):
            key_at = jnp.where(column >= slot * rrow, column + (scalar_ref[1 + slot] - rank - slot) * rrow, key_at)

        def forward(step):
            span = slice(step * block, (step + 1) * block)
            row = (step * block + lax.broadcasted_iota(jnp.int32, (block, 1), 0)) // per
            q = q_ref[span, :]
            s_p = dot_nt(q, k_s[:prompt_total, :])
            s_r = dot_nt(q, k_s[prompt_total:, :])
            s_r = jnp.where(key_at <= row, s_r, -jnp.inf)
            top = jnp.maximum(jnp.max(s_p, axis=1, keepdims=True), jnp.max(s_r, axis=1, keepdims=True))
            e_p = jnp.exp2((s_p - top) * exponent)
            e_r = jnp.exp2((s_r - top) * exponent)
            sums = jnp.sum(e_p, axis=1, keepdims=True) + jnp.sum(e_r, axis=1, keepdims=True)
            p_p = e_p.astype(BF16)
            p_r = e_r.astype(BF16)
            o = (dot_nn(p_p, v_s[:prompt_total, :]) + dot_nn(p_r, v_s[prompt_total:, :])) / sums
            there = slice((step - first) * block, (step - first + 1) * block)
            out_ref[there, :] = jnp.where(row < live, o, 0.0).astype(BF16)
            cot = (do_ref[span, :].astype(F32) * (scale / sums)).astype(BF16)
            cot32 = cot.astype(F32)
            off = jnp.sum(cot32 * o, axis=1, keepdims=True)
            q_t = q.astype(F32).T.astype(BF16)
            cot_t = cot32.T.astype(BF16)
            return p_p, p_r, cot, off, q_t, cot_t

        def backward(step, state):
            there = slice((step - first) * block, (step - first + 1) * block)
            p_p, p_r, cot, off, q_t, cot_t = state
            dv_s[:, :prompt_total] += dot_nn(cot_t, p_p)
            dv_s[:, prompt_total:] += dot_nn(cot_t, p_r)
            ds_p = (p_p.astype(F32) * (dot_nt(cot, v_s[:prompt_total, :]) - off)).astype(BF16)
            ds_r = (p_r.astype(F32) * (dot_nt(cot, v_s[prompt_total:, :]) - off)).astype(BF16)
            ds_ref[there, :prompt_total] = ds_p
            ds_ref[there, prompt_total:] = ds_r
            dk_s[:, :prompt_total] += dot_nn(q_t, ds_p)
            dk_s[:, prompt_total:] += dot_nn(q_t, ds_r)

        state = forward(first)
        for step in range(first, end):
            ahead = forward(step + 1) if step + 1 < end else None
            backward(step, state)
            state = ahead
        if not closing:
            return

        dk = dk_s[...].T
        dv = dv_s[...].T * (1.0 / scale)
        for dx, ref in enumerate(line_refs):
            for slot in range(seq_size):
                lower = (dx * seq_size + slot) * prow
                at = 2 * slot * prow
                ref[at : at + prow, :] = dk[lower : lower + prow, :].astype(ref.dtype)
                ref[at + prow : at + 2 * prow, :] = dv[lower : lower + prow, :].astype(ref.dtype)
        for slot, ref in enumerate(grad_refs):
            lower = prompt_total + slot * rrow
            ref[:rrow, :] = dk[lower : lower + rrow, :].astype(ref.dtype)
            ref[rrow:, :] = dv[lower : lower + rrow, :].astype(ref.dtype)

    shapes = [((here, dim), BF16), ((here, total), BF16)]
    sums = [((dim, total), F32)] * 2
    if opening:
        shapes += [((total, dim), BF16)] * 2
    if closing:
        shapes += [((seq_size * 2 * prow, dim), BF16 if dx else F32) for dx in range(roll_size)]
        shapes += [((2 * rrow, dim), BF16 if slot else F32) for slot in range(seq_size)]
    else:
        shapes += sums
    outs = pl.pallas_call(
        body,
        out_shape=[jax.ShapeDtypeStruct(shape, kind) for shape, kind in shapes],
        in_specs=[SMEM] + [VMEM] * (2 + len(sources)),
        out_specs=[VMEM] * len(shapes),
        scratch_shapes=[pltpu.VMEM(shape, kind) for shape, kind in sums] if closing else [],
        compiler_params=params(),
        cost_estimate=cost(20 * here * total * dim, 16 * here * dim, here * total),
    )(scalars, queries, cotangent, *sources)
    part, rest = tuple(outs[:2]), list(outs[2:])
    if not closing:
        return part, rest
    keys, rest = (rest[0], rest[2:]) if opening else (carry[0], rest)
    return part, keys, rest[:roll_size], rest[roll_size:]


def row_outputs(heads, keys, rows, block):
    groups = len(heads)
    total, dim = keys[0].shape
    flat = sum(out.shape[0] for out, _ in heads[0])
    per = flat // rows
    arrays = [item for head in heads for part in head for item in part]
    where, at = [], 0
    for head in heads:
        where.append([])
        for out, _ in head:
            where[-1] += [(at, lower) for lower in range(0, out.shape[0], block)]
            at += 2

    def body(*refs):
        part_refs, k_refs = refs[: len(arrays)], refs[len(arrays) : len(arrays) + groups]
        attention_ref, dq_ref = refs[len(arrays) + groups :]
        for i in range(flat // block):
            there = slice(i * block // per, (i + 1) * block // per)
            outs, grads = [], []
            for places, k in zip(where, k_refs):
                at, lower = places[i]
                span = slice(lower, lower + block)
                outs.append(part_refs[at][span, :].astype(F32).reshape(block // per, per, dim))
                grads.append(dot_nn(part_refs[at + 1][span, :], k[...]).reshape(block // per, per, dim))
            attention_ref[there] = jnp.concatenate(outs, axis=1).astype(BF16)
            dq_ref[there] = jnp.concatenate(grads, axis=1).astype(BF16)

    return pl.pallas_call(
        body,
        out_shape=[jax.ShapeDtypeStruct((rows, per * groups, dim), BF16)] * 2,
        in_specs=[VMEM] * (len(arrays) + groups),
        out_specs=[VMEM] * 2,
        compiler_params=params(),
        cost_estimate=cost(4 * groups * flat * total * dim, 2 * groups * flat * total),
    )(*arrays, *keys)


def pair_sum(owns, received, seq_size):
    groups = len(owns)
    rows, dim = owns[0].shape
    part = rows // seq_size
    count = len(received[0])

    def body(*refs):
        own_refs, other_refs, outs = refs[:groups], refs[groups : groups * (1 + count)], refs[groups * (1 + count) :]
        for slot, out in enumerate(outs):
            span = slice(slot * part, (slot + 1) * part)
            for g, own_ref in enumerate(own_refs):
                value = own_ref[span, :]
                for other in other_refs[g * count : (g + 1) * count]:
                    value = value + other[span, :].astype(F32)
                out[g * part : (g + 1) * part, :] = value.astype(out.dtype)

    return pl.pallas_call(
        body,
        out_shape=[jax.ShapeDtypeStruct((groups * part, dim), BF16 if slot else F32) for slot in range(seq_size)],
        in_specs=[VMEM] * (groups * (1 + count)),
        out_specs=[VMEM] * seq_size,
        compiler_params=params(),
        cost_estimate=cost(groups * rows * dim, groups * rows * dim * 10),
    )(*owns, *[item for line in received for item in line])


def finish(owns, received, groups):
    each = groups // len(owns)
    dim = owns[0].shape[1]
    rows = owns[0].shape[0] // (2 * each)
    count = len(received[0])

    def body(*refs):
        own, rest = refs[: len(owns)], refs[len(owns) :]
        sums = []
        for g in range(groups):
            i, span = g // each, slice(g % each * 2 * rows, (g % each + 1) * 2 * rows)
            value = own[i][span, :]
            for other in rest[i * count : (i + 1) * count]:
                value = value + other[span, :].astype(F32)
            sums.append(value)
        for part, out in enumerate(refs[-2:]):
            pieces = [value[part * rows : (part + 1) * rows, None, :] for value in sums]
            out[...] = jnp.concatenate(pieces, axis=1).astype(BF16)

    flat = [item for line in received for item in line]
    return pl.pallas_call(
        body,
        out_shape=[jax.ShapeDtypeStruct((rows, groups, dim), BF16)] * 2,
        in_specs=[VMEM] * (len(owns) + len(flat)),
        out_specs=[VMEM] * 2,
        compiler_params=params(),
        cost_estimate=cost(2 * rows * groups * dim * count, 2 * rows * groups * dim * 10),
    )(*owns, *flat)


def after(value, *others):
    return lax.optimization_barrier((value, others))[0]


def local(queries, rollout_keys, rollout_values, prompt_keys, prompt_values, grad_out, lengths):
    seq_size, roll_size = lax.axis_size("seq"), lax.axis_size("roll")
    row_count, groups = queries.shape[1], prompt_keys.shape[1]
    flat = row_count * queries.shape[2] // groups
    rank = lax.axis_index("seq")
    paired = seq_size & (seq_size - 1) == 0
    slots = range(1, seq_size)
    origin = [(rank ^ slot) if paired else (rank - slot) % seq_size for slot in slots]
    scalars = jnp.stack([lengths[0] - rank * row_count, rank] + origin).astype(jnp.int32)

    def pairs(slot):
        return [(i, i ^ slot if paired else (i + slot) % seq_size) for i in range(seq_size)]

    def over_seq(value, which):
        return lax.ppermute(value, "seq", which)

    def give_back(value, slot):
        return over_seq(value, [(b, a) for a, b in pairs(slot)])

    def give_down(value, slot):
        return over_seq(value, [(b, a) for a, b in pairs(slot) if a < b])

    def over_roll(value, shift):
        return lax.ppermute(value, "roll", [(i, (i + shift) % roll_size) for i in range(roll_size)])

    own = split_heads(prompt_keys, prompt_values, rollout_keys[0], rollout_values[0])
    q_groups, cot_groups, kept = split_queries(scalars, queries[0], grad_out[0], groups, own)
    prows, rrows = 2 * prompt_keys.shape[0], 2 * row_count

    def send_over_seq(part, same):
        return [same] + [over_seq(part, pairs(slot)) for slot in slots]

    def send_over_roll(messages):
        line = jnp.concatenate([item[:prows] for item in messages], axis=0)
        return [line] + [over_roll(line, shift) for shift in range(1, roll_size)]

    messages = send_over_seq(own[0], kept[0])
    lines = send_over_roll(messages)
    block = math.gcd(flat, 256)
    steps = flat // block
    heads, all_keys, line_own, line_got, roll_own, roll_got, near = [], [], [], [], [], [], []
    for g in range(groups):
        prompts = [(item, slot * prows, prows) for item in lines for slot in range(seq_size)]
        rollouts = [(item, prows, rrows) for item in messages]
        if g + 1 < groups:
            messages = send_over_seq(after(own[g + 1], lines[0]), kept[g + 1])
        cuts = [0, steps // 2, steps] if g else [0, steps]
        parts, carry = [], []
        for start, stop in zip(cuts, cuts[1:]):
            if start:
                carry = [after(item, roll_got[g - 1]) for item in carry]
            part, *rest = attend(
                scalars, q_groups[g], cot_groups[g], prompts, rollouts, roll_size, block, start, stop, carry
            )
            parts.append(part)
            carry = rest[0]
        keys, line_grads, roll_grads = rest
        heads.append(parts)
        all_keys.append(keys)
        line_own.append(line_grads[0])
        line_got.append([over_roll(line_grads[shift], -shift) for shift in range(1, roll_size)])
        if g + 1 < groups:
            messages = [after(item, parts) for item in messages]
            lines = send_over_roll(messages)
            roll_grads = [after(item, lines[0]) for item in roll_grads]
        roll_own.append(roll_grads[0])
        near.append(roll_grads[1])
        roll_got.append([give_down(roll_grads[slot], slot) for slot in slots if slot > 1])

    came = give_down(jnp.concatenate(near, axis=0), 1)
    roll_got = [got + [came[g * rrows : (g + 1) * rrows]] for g, got in enumerate(roll_got)]
    sums = pair_sum(line_own, line_got, seq_size)
    attention_rows, grad_rows = row_outputs(heads, all_keys, row_count, block)
    grad_rk, grad_rv = finish(roll_own, roll_got, groups)
    grad_pk, grad_pv = finish([sums[0]], [[give_back(sums[slot], slot) for slot in slots]], groups)
    return attention_rows[None], grad_rows[None], grad_rk[None], grad_rv[None], grad_pk, grad_pv


def solution(mesh):
    rows = P("roll", "seq", "head", None)
    shared = P(("seq", "roll"), "head", None)
    return jax.shard_map(
        local,
        mesh=mesh,
        in_specs=(rows, rows, rows, shared, shared, rows, P("roll")),
        out_specs=(rows, rows, rows, rows, shared, shared),
        check_vma=False,
    )
```
